128 devices in a mesh: role: 2 (over z_hi), rad: 2 (over core), lat: 32 (over x, z_lo, y).
Axes of the slice: x: 4, y: 4, z: 4 (z_hi: 2, z_lo: 2; z = z_hi * 2 + z_lo), core: 2. Of those that a mesh axis runs over, the one named last changes fastest.
Arguments:
- temp_start: float32 [32, 512, 1024], P('rad', 'lat'), may hold values from 0 to 1
- visc_ref: float32 [32, 512, 1024], P('rad', 'lat'), may hold values from 0.3 to 3
- pinned: int32 [32, 512, 1024], P('rad', 'lat'), may hold values 0 or 1
- loads: float32 [2, 32, 512, 1024], P(None, 'rad', 'lat'), may hold values from -6 to 6
Outputs:
- solutions: float32 [2, 2, 32, 512, 1024], P('role', None, 'rad', 'lat')
The draws below stay inside these ranges and needn't reach their ends.
Inputs may be any that keep to these rules, and one draw needn't show every extreme that they name: `pinned`: 1 marks a cell held at rest in every solve.
All inputs are finite; a program needn't handle non-finite values. No bound on the sum of `pinned` on one device may be relied on, other than what follows from the above.
Results may differ from the reference program's by a relative error of at most 0.0001.
Values sent between devices are 32-bit elements; how exact they have to be, the bound alone decides.
A program may use at most 128 MiB of HBM per device.

```python
import math
import jax
import jax.numpy as jnp

CB = 1024
SWEEPS = 8
NR = 32
NL = 512


def with_ends(array, stream_key, smallest, high):
    shape = array.shape
    spot = [jax.random.randint(jax.random.fold_in(stream_key, axis), (), 0, shape[axis]) for axis in range(len(shape))]
    array = array.at[tuple(spot)].set(smallest)
    longest = shape.index(max(shape))
    spot[longest] = (spot[longest] + 1) % shape[longest]
    return array.at[tuple(spot)].set(high)


def block_scale(own_key, dims, pieces, low, high):
    loudness, own = 1.0, jax.random.fold_in(own_key, 6)
    for dim, blocks in pieces:
        draws = jnp.exp(jax.random.uniform(jax.random.fold_in(own, dim), (blocks,), jnp.float32, low / len(pieces), high / len(pieces)))
        loudness = loudness * jnp.repeat(draws, dims[dim] // blocks).reshape([-1 if axis == dim else 1 for axis in range(len(dims))])
    return loudness


def noise(rng, dims, width, reach, shards=(), held_as=jnp.bfloat16):
    result = width * jax.random.normal(rng, dims, jnp.float32)
    if shards:
        result = result * block_scale(rng, dims, shards, -0.22, 0.18)
    return jnp.clip(result, -reach, reach).astype(held_as)


def setup_inputs(seed: int = 0) -> dict:
    arg_keys = jax.random.split(jax.random.key(seed), 5)
    return {
        "temp_start": jnp.clip(1.0 * jax.random.uniform(arg_keys[0], (NR, NL, CB), jnp.float32) ** block_scale(arg_keys[0], (NR, NL, CB), ((0, 2), (1, 32)), -0.2, 0.2), 0.0, 1.0),
        "visc_ref": jnp.clip(jnp.exp(math.log(3.0) - 2.3025851 * jax.random.uniform(arg_keys[1], (NR, NL, CB), jnp.float32) ** block_scale(arg_keys[1], (NR, NL, CB), ((0, 2), (1, 32)), -0.2, 0.2)), 0.3, 3.0),
        "pinned": with_ends((jax.random.randint(arg_keys[2], (NR, NL, CB), 0, 8) < 1).astype(jnp.int32), jax.random.fold_in(arg_keys[2], 1), 0, 1),
        "loads": noise(arg_keys[3], (2, NR, NL, CB), 1.0, 6.0, ((1, 2), (2, 32)), jnp.float32),
    }


REACTION = 0.5
RAYLEIGH = 8.0
TIME_STEP = 0.1
SOFTENING = 2.0


def extend(field, margin):
    field = jnp.pad(field, ((margin, margin), (0, 0), (0, 0)))
    return jnp.concatenate([field[:, -margin:], field, field[:, :margin]], axis=1)


def couplings(viscosity):
    centre = viscosity[1:-1, 1:-1]
    shifted = jnp.pad(centre, ((0, 0), (0, 0), (1, 1)))
    couple = (0.5 * (centre + viscosity[2:, 1:-1]), 0.5 * (centre + viscosity[:-2, 1:-1]),
              0.5 * (centre + viscosity[1:-1, 2:]), 0.5 * (centre + viscosity[1:-1, :-2]),
              0.5 * (centre + shifted[:, :, 2:]), 0.5 * (centre + shifted[:, :, :-2]))
    diagonal = couple[0] + couple[1] + couple[2] + couple[3] + couple[4] + couple[5] + REACTION * centre
    return couple, diagonal


def jacobi_sweep(potential, couple, diagonal, forcing, movable):
    shifted = jnp.pad(potential[1:-1, 1:-1], ((0, 0), (0, 0), (1, 1)))
    summed = forcing + couple[0] * potential[2:, 1:-1] + couple[1] * potential[:-2, 1:-1]
    summed = summed + couple[2] * potential[1:-1, 2:] + couple[3] * potential[1:-1, :-2]
    summed = summed + couple[4] * shifted[:, :, 2:] + couple[5] * shifted[:, :, :-2]
    return movable * summed / (diagonal + 1.0 - movable)


def advance(temp, potential):
    centre = temp[1:-1, 1:-1]
    shifted = jnp.pad(centre, ((0, 0), (0, 0), (1, 1)))
    laplace = temp[2:, 1:-1] + temp[:-2, 1:-1] + temp[1:-1, 2:] + temp[1:-1, :-2]
    laplace = laplace + shifted[:, :, 2:] + shifted[:, :, :-2] - 6.0 * centre
    radial_speed = 0.5 * (potential[1:-1, 2:] - potential[1:-1, :-2])
    lateral_speed = -0.5 * (potential[2:, 1:-1] - potential[:-2, 1:-1])
    transport = radial_speed * 0.5 * (temp[2:, 1:-1] - temp[:-2, 1:-1])
    transport = transport + lateral_speed * 0.5 * (temp[1:-1, 2:] - temp[1:-1, :-2])
    return centre + TIME_STEP * (laplace - transport)


def stokes_solve(couple, diagonal, forcing, movable):
    potential = jnp.zeros_like(forcing)
    for repeat in range(SWEEPS):
        potential = jacobi_sweep(extend(potential, 1), couple, diagonal, forcing, movable)
    return potential


def reference(temp_start, visc_ref, pinned, loads):
    movable = 1.0 - pinned.astype(jnp.float32)
    visc_wide = extend(visc_ref, 1)
    temp = temp_start
    forward = []
    adjoint = []
    for step in range(2):
        temp_wide = extend(temp, 1)
        viscosity = visc_wide * jnp.exp(-SOFTENING * temp_wide)
        couple, diagonal = couplings(viscosity)
        forcing = RAYLEIGH * 0.5 * (temp_wide[1:-1, 2:] - temp_wide[1:-1, :-2])
        potential = stokes_solve(couple, diagonal, forcing, movable)
        forward.append(potential)
        adjoint.append(stokes_solve(couple, diagonal, loads[step], movable))
        if step == 0:
            temp = advance(temp_wide, extend(potential, 1))
    return jnp.stack([jnp.stack(forward), jnp.stack(adjoint)])
```

```python
import jax
import jax.numpy as jnp
from jax import lax
from jax.experimental import pallas as pl
from jax.experimental.pallas import tpu as pltpu
from jax.sharding import PartitionSpec as P

MESH = pl.DeviceIdType.MESH
TIME_STEP = 0.1
SOFTENING = 2.0
RAYLEIGH = 8.0

K = 4
H = K + 1
N = 16
ROWS = N + H + 1
LAYERS = N + 2 * H

T, V, M, L0, L1, F4, A4, F8, G4 = range(9)
DEPTH = {T: H, V: K, M: K - 1, L0: K - 1, L1: K - 1, F4: K, A4: K, F8: H, G4: K}
LEFT, RIGHT, CORE, CORNER_LEFT, CORNER_RIGHT = range(5)


def b_masks():
    lane = lax.broadcasted_iota(jnp.int32, (1, 8, 128), 2)
    sub = lax.broadcasted_iota(jnp.int32, (1, 8, 128), 1)
    first, last = lane == 0, lane == 127
    return first, last, first & (sub == 0), last & (sub == 7)


def above(x, last):
    rolled = pltpu.roll(x, 127, 2)
    return jnp.where(last, pltpu.roll(rolled, 7, 1), rolled)


def below(x, first):
    rolled = pltpu.roll(x, 1, 2)
    return jnp.where(first, pltpu.roll(rolled, 1, 1), rolled)


def kernel(
    temp_hbm, visc_hbm, pinned_hbm, loads_hbm, out_hbm,
    temp, visc, pinned, half, coef, weight, bias, ping, pong, mid, full, mid2,
    load0, load1, bias_a, mid_a, ping_a, pong_a, full_a,
    send_sem, recv_sem, in_sem, out_sem,
):
    role, rad, lat = (lax.axis_index(name) for name in ("role", "rad", "lat"))
    peers = lax.axis_size("lat")
    left = (role, rad, lax.rem(lat + peers - 1, peers))
    right = (role, rad, lax.rem(lat + 1, peers))
    core = (role, 1 - rad, lat)
    is_forward = role == 0
    own = 1 + (H - 1) * rad

    barrier = pltpu.get_barrier_semaphore()
    for device in (left, right, core):
        pl.semaphore_signal(barrier, inc=1, device_id=device, device_id_type=MESH)

    def arriving(source, buffer, which):
        return [
            pltpu.make_async_copy(
                source.at[:, :, pl.ds(128 * j, 128)],
                buffer.at[pl.ds(own, N), pl.ds(H, N), j, :],
                in_sem.at[which, j],
            )
            for j in range(8)
        ]

    loading = [
        arriving(temp_hbm, temp, 0),
        arriving(visc_hbm, visc, 1),
        arriving(pinned_hbm, pinned, 2),
    ]
    loading_adjoint = [
        arriving(loads_hbm.at[0], load0, 3),
        arriving(loads_hbm.at[1], load1, 4),
    ]
    for copies in loading:
        for copy in copies:
            copy.start()

    @pl.when(role == 1)
    def _():
        for copies in loading_adjoint:
            for copy in copies:
                copy.start()

    outside = (ROWS - 1) * rad
    zero_row = jnp.zeros((LAYERS, 8, 128), jnp.float32)
    for buffer in (temp, half, bias, ping, pong, mid, full, mid2, bias_a, mid_a, ping_a, pong_a):
        buffer[outside] = zero_row

    def remote(buffer, which, part, rows_from, rows_to, rows, l_from, l_to, layers, device):
        return pltpu.make_async_remote_copy(
            src_ref=buffer.at[pl.ds(rows_from, rows), pl.ds(l_from, layers)],
            dst_ref=buffer.at[pl.ds(rows_to, rows), pl.ds(l_to, layers)],
            send_sem=send_sem.at[which, part],
            recv_sem=recv_sem.at[which, part],
            device_id=device,
            device_id_type=MESH,
        )

    def margins(buffer, which):
        d = DEPTH[which]
        rows_from = (1 - rad) * (1 + N - d) + rad * H
        rows_to = (1 - rad) * (H - d) + rad * (1 + N)
        return (
            remote(buffer, which, LEFT, own, own, N, H, H + N, d, left),
            remote(buffer, which, RIGHT, own, own, N, H + N - d, H - d, d, right),
            remote(buffer, which, CORE, rows_from, rows_to, d, H, H, N, core),
            remote(buffer, which, CORNER_LEFT, rows_from, rows_to, d, H - d, H - d, d, core),
            remote(buffer, which, CORNER_RIGHT, rows_from, rows_to, d, H + N, H + N, d, core),
        )

    moves = {
        which: margins(buffer, which)
        for which, buffer in (
            (T, temp), (V, visc), (M, pinned), (L0, load0), (L1, load1),
            (F4, mid), (A4, mid_a), (F8, full), (G4, mid2),
        )
    }

    def send(which):
        for part in (LEFT, RIGHT, CORE):
            moves[which][part].start()

    def have_core(*these):
        for which in these:
            moves[which][CORE].wait_recv()

    def have_sides(*these):
        for which in these:
            for part, corner in ((RIGHT, CORNER_LEFT), (LEFT, CORNER_RIGHT)):
                moves[which][part].wait_recv()
                moves[which][corner].start()
        for which in these:
            for corner in (CORNER_LEFT, CORNER_RIGHT):
                moves[which][corner].wait_recv()

    def sent(*these):
        for which in these:
            for part in range(5):
                moves[which][part].wait_send()

    first, last, bottom, top = b_masks()

    def over(extra, spans, body):
        start = own - extra * rad

        def row(i, carry):
            for low, high in spans:
                l = low
                while l < high:
                    n = min(high - l, 8)
                    body(start + i, H + l, n)
                    l += n
            return carry

        lax.fori_loop(0, N + extra, row, 0)

    def sweep(source, target, forced, extra, spans):
        def body(r, l, n):
            here = pl.ds(l, n)
            centre = source[r, here]
            total = forced[r, here] + coef[0, r, here] * source[r + 1, here]
            total = total + coef[1, r, here] * source[r - 1, here]
            total = total + coef[2, r, here] * source[r, pl.ds(l + 1, n)]
            total = total + coef[3, r, here] * source[r, pl.ds(l - 1, n)]
            total = total + coef[4, r, here] * above(centre, last)
            total = total + coef[5, r, here] * below(centre, first)
            target[r, here] = total

        over(extra, spans, body)

    def halves(field, spans):
        def body(r, l, n):
            here = pl.ds(l, n)
            half[r, here] = 0.5 * visc[r, here] * jnp.exp(-SOFTENING * field[r, here])

        over(K, spans, body)

    def couplings(field, spans, pick):
        def body(r, l, n):
            here = pl.ds(l, n)
            centre = half[r, here]
            around = (
                half[r + 1, here],
                half[r - 1, here],
                half[r, pl.ds(l + 1, n)],
                half[r, pl.ds(l - 1, n)],
                jnp.where(top, 0.0, above(centre, last)),
                jnp.where(bottom, 0.0, below(centre, first)),
            )
            diagonal = 7.0 * centre
            for other in around:
                diagonal = diagonal + other
            held = pinned[r, here].astype(jnp.float32)
            scale = (1.0 - held) / (diagonal + held)
            for i, other in enumerate(around):
                value = scale * (centre + other)
                if i == 4:
                    value = jnp.where(top, 0.0, value)
                if i == 5:
                    value = jnp.where(bottom, 0.0, value)
                coef[i, r, here] = value
            forcing = (0.5 * RAYLEIGH) * (field[r, pl.ds(l + 1, n)] - field[r, pl.ds(l - 1, n)])
            if pick:
                forcing = jnp.where(is_forward, forcing, load1[r, here])
            else:
                weight[r, here] = scale
            bias[r, here] = scale * forcing

        over(K - 1, spans, body)

    def adjoint_bias(spans):
        def body(r, l, n):
            here = pl.ds(l, n)
            bias_a[r, here] = weight[r, here] * load0[r, here]

        over(K - 1, spans, body)

    def advance(target, spans):
        def body(r, l, n):
            here, up, down = pl.ds(l, n), pl.ds(l + 1, n), pl.ds(l - 1, n)
            centre = temp[r, here]
            r_up, r_down = temp[r + 1, here], temp[r - 1, here]
            l_up, l_down = temp[r, up], temp[r, down]
            laplace = r_up + r_down + l_up + l_down
            laplace = laplace + jnp.where(top, 0.0, above(centre, last))
            laplace = laplace + jnp.where(bottom, 0.0, below(centre, first)) - 6.0 * centre
            radial = full[r, up] - full[r, down]
            lateral = full[r + 1, here] - full[r - 1, here]
            transport = 0.25 * (radial * (r_up - r_down) - lateral * (l_up - l_down))
            target[r, here] = centre + TIME_STEP * (laplace - transport)

        over(K, spans, body)

    def middle(j, shift=0):
        return ((j + shift, N - j - shift),)

    def sides(j, shift=0):
        return ((j - K, j + shift), (N - j - shift, N + K - j))

    def first_half(x, y, result, forced, spans):
        for j, source, target in ((2, forced, x), (3, x, y), (4, y, result)):
            sweep(source, target, forced, K - j, spans(j))

    def second_half(begin, x, y, result, forced, spans):
        for j, source, target in ((1, begin, x), (2, x, y), (3, y, x), (4, x, result)):
            sweep(source, target, forced, K - j, spans(j))

    def writing(buffer, which):
        return pltpu.make_async_copy(
            buffer.at[pl.ds(own, N), pl.ds(H, N)], out_hbm.at[which], out_sem.at[which]
        )

    pl.semaphore_wait(barrier, 3)
    for copies, which in zip(loading, (T, V, M)):
        for copy in copies:
            copy.wait()
        send(which)

    @pl.when(role == 1)
    def _():
        for copies, which in zip(loading_adjoint, (L0, L1)):
            for copy in copies:
                copy.wait()
            send(which)

    have_core(T, V, M)
    halves(temp, ((0, N),))
    couplings(temp, middle(1), False)
    first_half(ping, pong, mid, bias, middle)

    @pl.when(role == 1)
    def _():
        have_core(L0, L1)
        adjoint_bias(middle(1))
        first_half(ping_a, pong_a, mid_a, bias_a, middle)

    have_sides(T, V, M)
    halves(temp, ((-K, 0), (N, N + K)))
    couplings(temp, sides(1), False)
    first_half(ping, pong, mid, bias, sides)
    send(F4)

    @pl.when(role == 1)
    def _():
        have_sides(L0, L1)
        adjoint_bias(sides(1))
        first_half(ping_a, pong_a, mid_a, bias_a, sides)
        send(A4)

    have_core(F4)
    second_half(mid, ping, pong, full, bias, middle)

    @pl.when(role == 1)
    def _():
        have_core(A4)
        second_half(mid_a, ping_a, pong_a, full_a, bias_a, middle)

    have_sides(F4)
    second_half(mid, ping, pong, full, bias, sides)
    send(F8)

    @pl.when(role == 0)
    def _():
        writing(full, 0).start()

    @pl.when(role == 1)
    def _():
        have_sides(A4)
        second_half(mid_a, ping_a, pong_a, full_a, bias_a, sides)
        writing(full_a, 0).start()
        sent(A4)

    sent(F4)
    temp_next = mid
    have_core(F8)
    advance(temp_next, middle(1))
    halves(temp_next, middle(1))
    couplings(temp_next, middle(2), True)
    first_half(ping, pong, mid2, bias, lambda j: middle(j, 1))
    have_sides(F8)
    advance(temp_next, ((-K, 1), (N - 1, N + K)))
    halves(temp_next, ((-K, 1), (N - 1, N + K)))
    couplings(temp_next, sides(1, 1), True)
    first_half(ping, pong, mid2, bias, lambda j: sides(j, 1))
    send(G4)
    have_core(G4)
    final = mid_a
    second_half(mid2, ping, pong, final, bias, middle)
    have_sides(G4)
    second_half(mid2, ping, pong, final, bias, sides)
    writing(final, 1).start()
    sent(T, V, M, F8, G4)

    @pl.when(role == 1)
    def _():
        sent(L0, L1)

    writing(full, 0).wait()
    writing(final, 1).wait()


def per_device(temp_start, visc_ref, pinned, loads):
    field = pltpu.VMEM((ROWS, LAYERS, 8, 128), jnp.float32)
    scratch = [
        field, field, pltpu.VMEM((ROWS, LAYERS, 8, 128), jnp.int32), field,
        pltpu.VMEM((6, ROWS, LAYERS, 8, 128), jnp.float32),
    ] + [field] * 14 + [
        pltpu.SemaphoreType.DMA((9, 5)),
        pltpu.SemaphoreType.DMA((9, 5)),
        pltpu.SemaphoreType.DMA((5, 8)),
        pltpu.SemaphoreType.DMA((2,)),
    ]
    result = pl.pallas_call(
        kernel,
        out_shape=jax.ShapeDtypeStruct((2, N, N, 8, 128), jnp.float32),
        in_specs=[pl.BlockSpec(memory_space=pl.ANY)] * 4,
        out_specs=pl.BlockSpec(memory_space=pl.ANY),
        scratch_shapes=scratch,
        compiler_params=pltpu.CompilerParams(
            collective_id=0, has_side_effects=True, vmem_limit_bytes=60 * 1024 * 1024
        ),
    )(temp_start, visc_ref, pinned, loads)
    return result.reshape(1, 2, N, N, 1024)


def solution(mesh):
    in_specs = (
        P("rad", "lat", None),
        P("rad", "lat", None),
        P("rad", "lat", None),
        P(None, "rad", "lat", None),
    )
    out_specs = P("role", None, "rad", "lat", None)
    return jax.shard_map(
        per_device, mesh=mesh, in_specs=in_specs, out_specs=out_specs, check_vma=False
    )
```

```python
import jax
import jax.numpy as jnp
from jax import lax
from jax.experimental import pallas as pl
from jax.experimental.pallas import tpu as pltpu
from jax.sharding import PartitionSpec as P

MESH = pl.DeviceIdType.MESH
TIME_STEP = 0.1
SOFTENING = 2.0
RAYLEIGH = 8.0

K = 4
H = K + 1
N = 16
ROWS = N + H + 1
LAYERS = N + 2 * H

T, V, M, L0, L1, F4, A4, F8, G4 = range(9)
DEPTH = {T: H, V: K, M: K - 1, L0: K - 1, L1: K - 1, F4: K, A4: K, F8: H, G4: K}
LEFT, RIGHT, CORE, CORNER_LEFT, CORNER_RIGHT = range(5)


def b_masks():
    lane = lax.broadcasted_iota(jnp.int32, (1, 8, 128), 2)
    sub = lax.broadcasted_iota(jnp.int32, (1, 8, 128), 1)
    first, last = lane == 0, lane == 127
    return first, last, first & (sub == 0), last & (sub == 7)


def above(x, last):
    rolled = pltpu.roll(x, 127, 2)
    return jnp.where(last, pltpu.roll(rolled, 7, 1), rolled)


def below(x, first):
    rolled = pltpu.roll(x, 1, 2)
    return jnp.where(first, pltpu.roll(rolled, 1, 1), rolled)


def kernel(
    temp_hbm, visc_hbm, pinned_hbm, loads_hbm, out_hbm,
    temp, visc, pinned, half, coef, weight, bias, ping, pong, mid, full, mid2,
    load0, load1, bias_a, mid_a, ping_a, pong_a, full_a,
    send_sem, recv_sem, in_sem, out_sem,
):
    role, rad, lat = (lax.axis_index(name) for name in ("role", "rad", "lat"))
    peers = lax.axis_size("lat")
    left = (role, rad, lax.rem(lat + peers - 1, peers))
    right = (role, rad, lax.rem(lat + 1, peers))
    core = (role, 1 - rad, lat)
    is_forward = role == 0
    own = 1 + (H - 1) * rad

    barrier = pltpu.get_barrier_semaphore()
    for device in (left, right, core):
        pl.semaphore_signal(barrier, inc=1, device_id=device, device_id_type=MESH)

    def arriving(source, buffer, which):
        return [
            pltpu.make_async_copy(
                source.at[:, :, pl.ds(128 * j, 128)],
                buffer.at[pl.ds(own, N), pl.ds(H, N), j, :],
                in_sem.at[which, j],
            )
            for j in range(8)
        ]

    loading = [
        arriving(temp_hbm, temp, 0),
        arriving(visc_hbm, visc, 1),
        arriving(pinned_hbm, pinned, 2),
    ]
    loading_adjoint = [
        arriving(loads_hbm.at[0], load0, 3),
        arriving(loads_hbm.at[1], load1, 4),
    ]
    for copies in loading:
        for copy in copies:
            copy.start()

    @pl.when(role == 1)
    def _():
        for copies in loading_adjoint:
            for copy in copies:
                copy.start()

    outside = (ROWS - 1) * rad
    zero_row = jnp.zeros((LAYERS, 8, 128), jnp.float32)
    for buffer in (temp, half, bias, ping, pong, mid, full, mid2, bias_a, mid_a, ping_a, pong_a):
        buffer[outside] = zero_row

    def remote(buffer, which, part, rows_from, rows_to, rows, l_from, l_to, layers, device):
        return pltpu.make_async_remote_copy(
            src_ref=buffer.at[pl.ds(rows_from, rows), pl.ds(l_from, layers)],
            dst_ref=buffer.at[pl.ds(rows_to, rows), pl.ds(l_to, layers)],
            send_sem=send_sem.at[which, part],
            recv_sem=recv_sem.at[which, part],
            device_id=device,
            device_id_type=MESH,
        )

    def margins(buffer, which):
        d = DEPTH[which]
        rows_from = (1 - rad) * (1 + N - d) + rad * H
        rows_to = (1 - rad) * (H - d) + rad * (1 + N)
        return (
            remote(buffer, which, LEFT, own, own, N, H, H + N, d, left),
            remote(buffer, which, RIGHT, own, own, N, H + N - d, H - d, d, right),
            remote(buffer, which, CORE, rows_from, rows_to, d, H, H, N, core),
            remote(buffer, which, CORNER_LEFT, rows_from, rows_to, d, H - d, H - d, d, core),
            remote(buffer, which, CORNER_RIGHT, rows_from, rows_to, d, H + N, H + N, d, core),
        )

    moves = {
        which: margins(buffer, which)
        for which, buffer in (
            (T, temp), (V, visc), (M, pinned), (L0, load0), (L1, load1),
            (F4, mid), (A4, mid_a), (F8, full), (G4, mid2),
        )
    }

    def send(which):
        for part in (LEFT, RIGHT, CORE):
            moves[which][part].start()

    def have_core(*these):
        for which in these:
            moves[which][CORE].wait_recv()

    def have_sides(*these):
        for which in these:
            for part, corner in ((RIGHT, CORNER_LEFT), (LEFT, CORNER_RIGHT)):
                moves[which][part].wait_recv()
                moves[which][corner].start()
        for which in these:
            for corner in (CORNER_LEFT, CORNER_RIGHT):
                moves[which][corner].wait_recv()

    def sent(*these):
        for which in these:
            for part in range(5):
                moves[which][part].wait_send()

    first, last, bottom, top = b_masks()

    def over(extra, spans, body):
        extra = (0, 2, 2, 4, 4)[extra]
        group = (N + extra) // 2
        start = own - extra * rad

        def rows(g, carry):
            def row(i, inner):
                for low, high in spans:
                    l = low
                    while l < high:
                        n = min(high - l, 8)
                        body(start + g * group + i, H + l, n)
                        l += n
                return inner

            return lax.fori_loop(0, group, row, carry, unroll=True)

        lax.fori_loop(0, 2, rows, 0)

    def sweep(source, target, forced, extra, spans):
        def body(r, l, n):
            here = pl.ds(l, n)
            centre = source[r, here]
            total = forced[r, here] + coef[0, r, here] * source[r + 1, here]
            total = total + coef[1, r, here] * source[r - 1, here]
            total = total + coef[2, r, here] * source[r, pl.ds(l + 1, n)]
            total = total + coef[3, r, here] * source[r, pl.ds(l - 1, n)]
            total = total + coef[4, r, here] * above(centre, last)
            total = total + coef[5, r, here] * below(centre, first)
            target[r, here] = total

        over(extra, spans, body)

    def halves(field, spans):
        def body(r, l, n):
            here = pl.ds(l, n)
            half[r, here] = 0.5 * visc[r, here] * jnp.exp(-SOFTENING * field[r, here])

        over(K, spans, body)

    def couplings(field, spans, pick):
        def body(r, l, n):
            here = pl.ds(l, n)
            centre = half[r, here]
            around = (
                half[r + 1, here],
                half[r - 1, here],
                half[r, pl.ds(l + 1, n)],
                half[r, pl.ds(l - 1, n)],
                jnp.where(top, 0.0, above(centre, last)),
                jnp.where(bottom, 0.0, below(centre, first)),
            )
            diagonal = 7.0 * centre
            for other in around:
                diagonal = diagonal + other
            held = pinned[r, here].astype(jnp.float32)
            scale = (1.0 - held) / (diagonal + held)
            for i, other in enumerate(around):
                value = scale * (centre + other)
                if i == 4:
                    value = jnp.where(top, 0.0, value)
                if i == 5:
                    value = jnp.where(bottom, 0.0, value)
                coef[i, r, here] = value
            forcing = (0.5 * RAYLEIGH) * (field[r, pl.ds(l + 1, n)] - field[r, pl.ds(l - 1, n)])
            if pick:
                forcing = jnp.where(is_forward, forcing, load1[r, here])
            else:
                weight[r, here] = scale
            bias[r, here] = scale * forcing

        over(K - 1, spans, body)

    def adjoint_bias(spans):
        def body(r, l, n):
            here = pl.ds(l, n)
            bias_a[r, here] = weight[r, here] * load0[r, here]

        over(K - 1, spans, body)

    def advance(target, spans):
        def body(r, l, n):
            here, up, down = pl.ds(l, n), pl.ds(l + 1, n), pl.ds(l - 1, n)
            centre = temp[r, here]
            r_up, r_down = temp[r + 1, here], temp[r - 1, here]
            l_up, l_down = temp[r, up], temp[r, down]
            laplace = r_up + r_down + l_up + l_down
            laplace = laplace + jnp.where(top, 0.0, above(centre, last))
            laplace = laplace + jnp.where(bottom, 0.0, below(centre, first)) - 6.0 * centre
            radial = full[r, up] - full[r, down]
            lateral = full[r + 1, here] - full[r - 1, here]
            transport = 0.25 * (radial * (r_up - r_down) - lateral * (l_up - l_down))
            target[r, here] = centre + TIME_STEP * (laplace - transport)

        over(K, spans, body)

    def middle(j, shift=0):
        return ((j + shift, N - j - shift),)

    def sides(j, shift=0):
        return ((j - K, j + shift), (N - j - shift, N + K - j))

    def first_half(x, y, result, forced, spans):
        for j, source, target in ((2, forced, x), (3, x, y), (4, y, result)):
            sweep(source, target, forced, K - j, spans(j))

    def second_half(begin, x, y, result, forced, spans):
        for j, source, target in ((1, begin, x), (2, x, y), (3, y, x), (4, x, result)):
            sweep(source, target, forced, K - j, spans(j))

    def writing(buffer, which):
        return pltpu.make_async_copy(
            buffer.at[pl.ds(own, N), pl.ds(H, N)], out_hbm.at[which], out_sem.at[which]
        )

    pl.semaphore_wait(barrier, 3)
    for copies, which in zip(loading, (T, V, M)):
        for copy in copies:
            copy.wait()
        send(which)

    @pl.when(role == 1)
    def _():
        for copies, which in zip(loading_adjoint, (L0, L1)):
            for copy in copies:
                copy.wait()
            send(which)

    have_core(T, V, M)
    halves(temp, ((0, N),))
    couplings(temp, middle(1), False)
    first_half(ping, pong, mid, bias, middle)

    @pl.when(role == 1)
    def _():
        have_core(L0, L1)
        adjoint_bias(middle(1))
        first_half(ping_a, pong_a, mid_a, bias_a, middle)

    have_sides(T, V, M)
    halves(temp, ((-K, 0), (N, N + K)))
    couplings(temp, sides(1), False)
    first_half(ping, pong, mid, bias, sides)
    send(F4)

    @pl.when(role == 1)
    def _():
        have_sides(L0, L1)
        adjoint_bias(sides(1))
        first_half(ping_a, pong_a, mid_a, bias_a, sides)
        send(A4)

    have_core(F4)
    second_half(mid, ping, pong, full, bias, middle)

    @pl.when(role == 1)
    def _():
        have_core(A4)
        second_half(mid_a, ping_a, pong_a, full_a, bias_a, middle)

    have_sides(F4)
    second_half(mid, ping, pong, full, bias, sides)
    send(F8)

    @pl.when(role == 0)
    def _():
        writing(full, 0).start()

    @pl.when(role == 1)
    def _():
        have_sides(A4)
        second_half(mid_a, ping_a, pong_a, full_a, bias_a, sides)
        writing(full_a, 0).start()
        sent(A4)

    sent(F4)
    temp_next = mid
    have_core(F8)
    advance(temp_next, middle(1))
    halves(temp_next, middle(1))
    couplings(temp_next, middle(2), True)
    first_half(ping, pong, mid2, bias, lambda j: middle(j, 1))
    have_sides(F8)
    advance(temp_next, ((-K, 1), (N - 1, N + K)))
    halves(temp_next, ((-K, 1), (N - 1, N + K)))
    couplings(temp_next, sides(1, 1), True)
    first_half(ping, pong, mid2, bias, lambda j: sides(j, 1))
    send(G4)
    have_core(G4)
    final = mid_a
    second_half(mid2, ping, pong, final, bias, middle)
    have_sides(G4)
    second_half(mid2, ping, pong, final, bias, sides)
    writing(final, 1).start()
    sent(T, V, M, F8, G4)

    @pl.when(role == 1)
    def _():
        sent(L0, L1)

    writing(full, 0).wait()
    writing(final, 1).wait()


def per_device(temp_start, visc_ref, pinned, loads):
    field = pltpu.VMEM((ROWS, LAYERS, 8, 128), jnp.float32)
    scratch = [
        field, field, pltpu.VMEM((ROWS, LAYERS, 8, 128), jnp.int32), field,
        pltpu.VMEM((6, ROWS, LAYERS, 8, 128), jnp.float32),
    ] + [field] * 14 + [
        pltpu.SemaphoreType.DMA((9, 5)),
        pltpu.SemaphoreType.DMA((9, 5)),
        pltpu.SemaphoreType.DMA((5, 8)),
        pltpu.SemaphoreType.DMA((2,)),
    ]
    result = pl.pallas_call(
        kernel,
        out_shape=jax.ShapeDtypeStruct((2, N, N, 8, 128), jnp.float32),
        in_specs=[pl.BlockSpec(memory_space=pl.ANY)] * 4,
        out_specs=pl.BlockSpec(memory_space=pl.ANY),
        scratch_shapes=scratch,
        compiler_params=pltpu.CompilerParams(
            collective_id=0, has_side_effects=True, vmem_limit_bytes=60 * 1024 * 1024
        ),
    )(temp_start, visc_ref, pinned, loads)
    return result.reshape(1, 2, N, N, 1024)


def solution(mesh):
    in_specs = (
        P("rad", "lat", None),
        P("rad", "lat", None),
        P("rad", "lat", None),
        P(None, "rad", "lat", None),
    )
    out_specs = P("role", None, "rad", "lat", None)
    return jax.shard_map(
        per_device, mesh=mesh, in_specs=in_specs, out_specs=out_specs, check_vma=False
    )
```

```python
import jax
import jax.numpy as jnp
from jax import lax
from jax.experimental import pallas as pl
from jax.experimental.pallas import tpu as pltpu
from jax.sharding import PartitionSpec as P

MESH = pl.DeviceIdType.MESH
TIME_STEP = 0.1
SOFTENING = 2.0
RAYLEIGH = 8.0

K = 4
H = K + 1
N = 16
ROWS = N + H + 1

T, V, M, L0, L1, F4, A4, F8, G4 = range(9)
DEPTH = {T: H, V: K, M: K - 1, L0: K - 1, L1: K - 1, F4: K, A4: K, F8: H, G4: K}
STEPS = (12, 8, 4, 0)
WHOLE = (0,)
CHUNKS = {T: (11, 8, 4, 0), V: STEPS, M: STEPS, L0: WHOLE, L1: WHOLE, F4: STEPS, A4: WHOLE, F8: STEPS, G4: STEPS}
CORE, CORNER_LEFT, CORNER_RIGHT, LEFT, RIGHT = 0, 1, 2, 3, 7


def b_masks():
    lane = lax.broadcasted_iota(jnp.int32, (1, 8, 128), 2)
    sub = lax.broadcasted_iota(jnp.int32, (1, 8, 128), 1)
    first, last = lane == 0, lane == 127
    return first, last, first & (sub == 0), last & (sub == 7)


def above(x, last):
    rolled = pltpu.roll(x, 127, 2)
    return jnp.where(last, pltpu.roll(rolled, 7, 1), rolled)


def below(x, first):
    rolled = pltpu.roll(x, 1, 2)
    return jnp.where(first, pltpu.roll(rolled, 1, 1), rolled)


class Field:
    def __init__(self, ref, margin):
        self.ref, self.margin = ref, margin

    def get(self, r, l, n):
        return self.ref[r, pl.ds(self.margin + l, n)]

    def put(self, r, l, value):
        self.ref[r, pl.ds(self.margin + l, value.shape[0])] = value

    def view(self, r, rows, l, layers):
        return self.ref.at[pl.ds(r, rows), pl.ds(self.margin + l, layers)]


MARGINS = (
    ("temp", H), ("visc", K), ("pinned", 3), ("half", K), ("weight", 3), ("bias", 3), ("ping", 3), ("pong", 3),
    ("mid", K), ("full", H), ("mid2", K), ("load0", 3), ("load1", 3), ("bias_a", 3), ("mid_a", K),
    ("ping_a", 3), ("pong_a", 3), ("full_a", 0),
)


def kernel(temp_hbm, visc_hbm, pinned_hbm, loads_hbm, out_hbm, *scratch):
    fields = {name: Field(ref, margin) for (name, margin), ref in zip(MARGINS, scratch)}
    coef1, coef2, send_sem, recv_sem, in_sem, out_sem = scratch[len(MARGINS):]
    temp, visc, pinned, half, weight, bias, ping, pong, mid, full, mid2 = (
        fields[name] for name, _ in MARGINS[:11]
    )
    load0, load1, bias_a, mid_a, ping_a, pong_a, full_a = (fields[name] for name, _ in MARGINS[11:])

    role, rad, lat = (lax.axis_index(name) for name in ("role", "rad", "lat"))
    peers = lax.axis_size("lat")
    left = (role, rad, lax.rem(lat + peers - 1, peers))
    right = (role, rad, lax.rem(lat + 1, peers))
    core = (role, 1 - rad, lat)
    is_forward = role == 0
    own = 1 + (H - 1) * rad

    barrier = pltpu.get_barrier_semaphore()
    for device in (left, right, core):
        pl.semaphore_signal(barrier, inc=1, device_id=device, device_id_type=MESH)

    def arriving(source, field, which):
        return [
            pltpu.make_async_copy(
                source.at[:, :, pl.ds(128 * j, 128)],
                field.ref.at[pl.ds(own, N), pl.ds(field.margin, N), j, :],
                in_sem.at[which, j],
            )
            for j in range(8)
        ]

    loading = [
        arriving(temp_hbm, temp, 0),
        arriving(visc_hbm, visc, 1),
        arriving(pinned_hbm, pinned, 2),
    ]
    loading_adjoint = [
        arriving(loads_hbm.at[1], load1, 3),
        arriving(loads_hbm.at[0], load0, 4),
    ]
    for copies in loading:
        for copy in copies:
            copy.start()

    @pl.when(role == 1)
    def _():
        for copies in loading_adjoint:
            for copy in copies:
                copy.start()

    outside = (ROWS - 1) * rad
    for field in (temp, half, bias, ping, pong, mid, full, mid2, bias_a, mid_a, ping_a, pong_a):
        field.ref[outside] = jnp.zeros((N + 2 * field.margin, 8, 128), jnp.float32)

    def first_row(low, high):
        return own + (1 - rad) * low + rad * (N - high)

    def remote(field, which, part, rows_from, rows_to, rows, l_from, l_to, layers, device):
        return pltpu.make_async_remote_copy(
            src_ref=field.view(rows_from, rows, l_from, layers),
            dst_ref=field.view(rows_to, rows, l_to, layers),
            send_sem=send_sem.at[which, part],
            recv_sem=recv_sem.at[which, part],
            device_id=device,
            device_id_type=MESH,
        )

    def margins(field, which):
        d = DEPTH[which]
        rows_from = (1 - rad) * (1 + N - d) + rad * H
        rows_to = (1 - rad) * (H - d) + rad * (1 + N)
        parts = {
            CORE: remote(field, which, CORE, rows_from, rows_to, d, 0, 0, N, core),
            CORNER_LEFT: remote(field, which, CORNER_LEFT, rows_from, rows_to, d, -d, -d, d, core),
            CORNER_RIGHT: remote(field, which, CORNER_RIGHT, rows_from, rows_to, d, N, N, d, core),
        }
        high = N
        for i, low in enumerate(CHUNKS[which]):
            row, rows = first_row(low, high), high - low
            parts[LEFT + i] = remote(field, which, LEFT + i, row, row, rows, 0, N, d, left)
            parts[RIGHT + i] = remote(field, which, RIGHT + i, row, row, rows, N - d, -d, d, right)
            high = low
        return parts

    moves = {
        which: margins(field, which)
        for which, field in (
            (T, temp), (V, visc), (M, pinned), (L0, load0), (L1, load1),
            (F4, mid), (A4, mid_a), (F8, full), (G4, mid2),
        )
    }

    def send_core(which):
        moves[which][CORE].start()

    def send_chunk(which, i):
        moves[which][LEFT + i].start()
        moves[which][RIGHT + i].start()

    def have_core(*these):
        for which in these:
            moves[which][CORE].wait_recv()

    def have_chunk(i, *these):
        for which in these:
            moves[which][LEFT + i].wait_recv()
            moves[which][RIGHT + i].wait_recv()

    def send_corners(*these):
        for which in these:
            moves[which][CORNER_LEFT].start()
            moves[which][CORNER_RIGHT].start()

    def have_corners(*these):
        for which in these:
            moves[which][CORNER_LEFT].wait_recv()
            moves[which][CORNER_RIGHT].wait_recv()

    def have_sides(which):
        have_chunk(0, which)
        send_corners(which)
        have_corners(which)

    def sent(*these):
        for which in these:
            for move in moves[which].values():
                move.wait_send()

    first, last, bottom, top = b_masks()

    def over(low, high, spans, body):
        if high - low <= 11:
            groups = 1
        else:
            groups = 2
            high += (high - low) % 2
        group = (high - low) // groups
        start = first_row(low, high)

        def rows(g, carry):
            def row(i, inner):
                for begin, end in spans:
                    l = begin
                    while l < end:
                        n = min(end - l, 8)
                        body(start + g * group + i, l, n)
                        l += n
                return inner

            return lax.fori_loop(0, group, row, carry, unroll=True)

        if groups == 1:
            rows(0, 0)
        else:
            lax.fori_loop(0, groups, rows, 0)

    def sweep(source, target, forced, coef, spans):
        def body(r, l, n):
            here = pl.ds(3 + l, n)
            centre = source.get(r, l, n)
            total = forced.get(r, l, n) + coef[0, r, here] * source.get(r + 1, l, n)
            total = total + coef[1, r, here] * source.get(r - 1, l, n)
            total = total + coef[2, r, here] * source.get(r, l + 1, n)
            total = total + coef[3, r, here] * source.get(r, l - 1, n)
            total = total + coef[4, r, here] * above(centre, last)
            total = total + coef[5, r, here] * below(centre, first)
            target.put(r, l, total)

        return lambda low, high: over(low, high, spans, body)

    def halves(field, spans):
        def body(r, l, n):
            half.put(r, l, 0.5 * visc.get(r, l, n) * jnp.exp(-SOFTENING * field.get(r, l, n)))

        return lambda low, high: over(low, high, spans, body)

    def couplings(field, coef, spans, pick):
        def body(r, l, n):
            here = pl.ds(3 + l, n)
            centre = half.get(r, l, n)
            around = (
                half.get(r + 1, l, n),
                half.get(r - 1, l, n),
                half.get(r, l + 1, n),
                half.get(r, l - 1, n),
                jnp.where(top, 0.0, above(centre, last)),
                jnp.where(bottom, 0.0, below(centre, first)),
            )
            diagonal = 7.0 * centre
            for other in around:
                diagonal = diagonal + other
            held = pinned.get(r, l, n).astype(jnp.float32)
            scale = (1.0 - held) / (diagonal + held)
            for i, other in enumerate(around):
                value = scale * (centre + other)
                if i == 4:
                    value = jnp.where(top, 0.0, value)
                if i == 5:
                    value = jnp.where(bottom, 0.0, value)
                coef[i, r, here] = value
            forcing = (0.5 * RAYLEIGH) * (field.get(r, l + 1, n) - field.get(r, l - 1, n))
            if pick:
                forcing = jnp.where(is_forward, forcing, load1.get(r, l, n))
            else:
                weight.put(r, l, scale)
            bias.put(r, l, scale * forcing)

        return lambda low, high: over(low, high, spans, body)

    def adjoint_bias(spans):
        def body(r, l, n):
            bias_a.put(r, l, weight.get(r, l, n) * load0.get(r, l, n))

        return lambda low, high: over(low, high, spans, body)

    def advance(target, spans):
        def body(r, l, n):
            centre = temp.get(r, l, n)
            r_up, r_down = temp.get(r + 1, l, n), temp.get(r - 1, l, n)
            l_up, l_down = temp.get(r, l + 1, n), temp.get(r, l - 1, n)
            laplace = r_up + r_down + l_up + l_down
            laplace = laplace + jnp.where(top, 0.0, above(centre, last))
            laplace = laplace + jnp.where(bottom, 0.0, below(centre, first)) - 6.0 * centre
            radial = full.get(r, l + 1, n) - full.get(r, l - 1, n)
            lateral = full.get(r + 1, l, n) - full.get(r - 1, l, n)
            transport = 0.25 * (radial * (r_up - r_down) - lateral * (l_up - l_down))
            target.put(r, l, centre + TIME_STEP * (laplace - transport))

        return lambda low, high: over(low, high, spans, body)

    def middle(j, shift=0):
        return ((j + shift, N - j - shift),)

    def sides(j, shift=0):
        return ((j - K, j + shift), (N - j - shift, N + K - j))

    def first_half(x, y, result, forced, coef, spans, lag):
        return [
            (sweep(source, target, forced, coef, spans(j)), lag + j, N + K - j)
            for j, source, target in ((2, forced, x), (3, x, y), (4, y, result))
        ]

    def second_half(begin, x, y, result, forced, coef, spans):
        return [
            (sweep(source, target, forced, coef, spans(j)), j, N + K - j)
            for j, source, target in ((1, begin, x), (2, x, y), (3, y, x), (4, x, result))
        ]

    def all_rows(stage):
        for work, _, high in stage:
            work(0, high)

    def wave(stage, arrive, leave):
        highs = [high for _, _, high in stage]
        for i, low in enumerate(STEPS):
            arrive(i)
            if i == 0:
                continue
            for place, (work, lag, _) in enumerate(stage):
                begin = min(low + lag, highs[place]) if low else 0
                if begin < highs[place]:
                    work(begin, highs[place])
                    highs[place] = begin
            leave(i)

    def writing(field, which, part, low, high):
        row = first_row(low, high)
        return pltpu.make_async_copy(
            field.view(row, high - low, 0, N),
            out_hbm.at[which, pl.ds(row - own, high - low)],
            out_sem.at[which, part],
        )

    for copies in loading:
        for copy in copies:
            copy.wait()
    pl.semaphore_wait(barrier, 3)
    for i in range(len(STEPS)):
        for which in (T, V, M):
            send_chunk(which, i)
        if i == 0:
            for which in (T, V, M):
                send_core(which)

    @pl.when(role == 1)
    def _():
        for copies in loading_adjoint:
            for copy in copies:
                copy.wait()
        send_chunk(L1, 0)
        send_core(L0)
        send_core(L1)

    have_core(T, V, M)
    all_rows(
        [(halves(temp, ((0, N),)), 0, N + K), (couplings(temp, coef1, middle(1), False), 1, N + K - 1)]
        + first_half(ping, pong, mid, bias, coef1, middle, 0)
    )

    def inputs_arrive(i):
        have_chunk(i, T, V, M)
        if i == 0:
            send_corners(T, V, M)
        if i == 1:
            have_corners(T, V, M)

    def leave_four(which):
        def leave(i):
            if i == 1:
                send_chunk(which, 0)
                send_core(which)
            if i == 2:
                send_chunk(which, 1)
            if i == 3:
                send_chunk(which, 2)
                send_chunk(which, 3)

        return leave

    wave(
        [(halves(temp, ((-K, 0), (N, N + K))), 0, N + K), (couplings(temp, coef1, sides(1), False), 1, N + K - 1)]
        + first_half(ping, pong, mid, bias, coef1, sides, 0),
        inputs_arrive,
        leave_four(F4),
    )

    @pl.when(role == 1)
    def _():
        send_chunk(L0, 0)

    have_core(F4)
    all_rows(second_half(mid, ping, pong, full, bias, coef1, middle))

    @pl.when(role == 1)
    def _():
        have_core(L0, L1)
        all_rows(
            [(adjoint_bias(middle(1)), 0, N + K - 1)]
            + first_half(ping_a, pong_a, mid_a, bias_a, coef1, middle, 0)
        )
        have_sides(L1)

    def potential_arrives(which):
        def arrive(i):
            have_chunk(i, which)
            if i == 0:
                send_corners(which)
            if i == 1:
                have_corners(which)

        return arrive

    def leave_full(i):
        if i == 1:
            send_chunk(F8, 0)
        if i == 2:
            send_chunk(F8, 1)
            send_core(F8)
        if i == 3:
            send_chunk(F8, 2)
            send_chunk(F8, 3)

    wave(second_half(mid, ping, pong, full, bias, coef1, sides), potential_arrives(F4), leave_full)

    @pl.when(role == 0)
    def _():
        writing(full, 0, 0, 0, N).start()

    @pl.when(role == 1)
    def _():
        have_sides(L0)
        all_rows(
            [(adjoint_bias(sides(1)), 0, N + K - 1)]
            + first_half(ping_a, pong_a, mid_a, bias_a, coef1, sides, 0)
        )
        send_chunk(A4, 0)
        send_core(A4)

    sent(F4)
    temp_next = mid
    have_core(F8)
    all_rows(
        [
            (advance(temp_next, middle(1)), 0, N + K),
            (halves(temp_next, middle(1)), 0, N + K),
            (couplings(temp_next, coef2, middle(2), True), 0, N + K - 1),
        ]
        + first_half(ping, pong, mid2, bias, coef2, lambda j: middle(j, 1), 0)
    )

    def full_arrives(i):
        have_chunk(i, F8)
        if i == 1:
            send_corners(F8)
            have_corners(F8)

    def leave_next(i):
        if i == 2:
            send_chunk(G4, 0)
            send_core(G4)
        if i == 3:
            send_chunk(G4, 1)
            send_chunk(G4, 2)
            send_chunk(G4, 3)

    wave(
        [
            (advance(temp_next, ((-K, 1), (N - 1, N + K))), 1, N + K),
            (halves(temp_next, ((-K, 1), (N - 1, N + K))), 1, N + K),
            (couplings(temp_next, coef2, sides(1, 1), True), 2, N + K - 1),
        ]
        + first_half(ping, pong, mid2, bias, coef2, lambda j: sides(j, 1), 1),
        full_arrives,
        leave_next,
    )
    final = temp
    sent(T, V, M)
    have_core(G4)
    all_rows(second_half(mid2, ping, pong, final, bias, coef2, middle))

    @pl.when(role == 1)
    def _():
        have_core(A4)
        all_rows(second_half(mid_a, ping_a, pong_a, full_a, bias_a, coef1, middle))
        have_sides(A4)
        all_rows(second_half(mid_a, ping_a, pong_a, full_a, bias_a, coef1, sides))
        writing(full_a, 0, 0, 0, N).start()

    def leave_final(i):
        if i == 2:
            writing(final, 1, 0, 8, N).start()
        if i == 3:
            writing(final, 1, 1, 0, 8).start()

    wave(second_half(mid2, ping, pong, final, bias, coef2, sides), potential_arrives(G4), leave_final)
    sent(F8, G4)

    @pl.when(role == 1)
    def _():
        sent(L0, L1, A4)

    writing(full, 0, 0, 0, N).wait()
    writing(final, 1, 0, 8, N).wait()
    writing(final, 1, 1, 0, 8).wait()


def per_device(temp_start, visc_ref, pinned, loads):
    def block(margin, dtype=jnp.float32, lead=()):
        return pltpu.VMEM(lead + (ROWS, N + 2 * margin, 8, 128), dtype)

    scratch = [block(margin, jnp.int32 if name == "pinned" else jnp.float32) for name, margin in MARGINS]
    scratch += [block(3, lead=(6,)), block(3, lead=(6,))]
    scratch += [
        pltpu.SemaphoreType.DMA((9, 11)),
        pltpu.SemaphoreType.DMA((9, 11)),
        pltpu.SemaphoreType.DMA((5, 8)),
        pltpu.SemaphoreType.DMA((2, 2)),
    ]
    result = pl.pallas_call(
        kernel,
        out_shape=jax.ShapeDtypeStruct((2, N, N, 8, 128), jnp.float32),
        in_specs=[pl.BlockSpec(memory_space=pl.ANY)] * 4,
        out_specs=pl.BlockSpec(memory_space=pl.ANY),
        scratch_shapes=scratch,
        compiler_params=pltpu.CompilerParams(
            collective_id=0, has_side_effects=True, vmem_limit_bytes=60 * 1024 * 1024
        ),
    )(temp_start, visc_ref, pinned, loads)
    return result.reshape(1, 2, N, N, 1024)


def solution(mesh):
    in_specs = (
        P("rad", "lat", None),
        P("rad", "lat", None),
        P("rad", "lat", None),
        P(None, "rad", "lat", None),
    )
    out_specs = P("role", None, "rad", "lat", None)
    return jax.shard_map(
        per_device, mesh=mesh, in_specs=in_specs, out_specs=out_specs, check_vma=False
    )
```

```python
import jax
import jax.numpy as jnp
from jax import lax
from jax.experimental import pallas as pl
from jax.experimental.pallas import tpu as pltpu
from jax.sharding import PartitionSpec as P

MESH = pl.DeviceIdType.MESH
TIME_STEP = 0.1
SOFTENING = 2.0
RAYLEIGH = 8.0

K = 4
H = K + 1
N = 16
ROWS = N + H + 1

T, V, M, L0, L1, F4, A4, F8, G4, FAR = range(10)
DEPTH = {T: K, V: K, M: K - 1, L0: K - 1, L1: K - 1, F4: K, A4: K, F8: H, G4: K, FAR: 1}
STEPS = (12, 6, 2, 0)
LATER = (12, 7, 2, 0)
WHOLE = (0,)
CHUNKS = {T: (11, 6, 2, 0), V: STEPS, M: STEPS, F4: STEPS, F8: STEPS, G4: LATER}
CORE, CORNER_LEFT, CORNER_RIGHT, LEFT, RIGHT = 0, 1, 2, 3, 7


def b_masks():
    lane = lax.broadcasted_iota(jnp.int32, (1, 8, 128), 2)
    sub = lax.broadcasted_iota(jnp.int32, (1, 8, 128), 1)
    first, last = lane == 0, lane == 127
    return first, last, first & (sub == 0), last & (sub == 7)


def above(x, last):
    rolled = pltpu.roll(x, 127, 2)
    return jnp.where(last, pltpu.roll(rolled, 7, 1), rolled)


def below(x, first):
    rolled = pltpu.roll(x, 1, 2)
    return jnp.where(first, pltpu.roll(rolled, 1, 1), rolled)


class Field:
    def __init__(self, ref, margin):
        self.ref, self.margin = ref, margin

    def get(self, r, l, n):
        return self.ref[r, pl.ds(self.margin + l, n)]

    def put(self, r, l, value):
        self.ref[r, pl.ds(self.margin + l, value.shape[0])] = value

    def view(self, r, rows, l, layers):
        return self.ref.at[pl.ds(r, rows), pl.ds(self.margin + l, layers)]


MARGINS = (
    ("temp", H), ("visc", K), ("pinned", 3), ("half", K), ("weight", 3), ("bias", 3), ("ping", 3), ("pong", 3),
    ("mid", K), ("full", H), ("mid2", K), ("load0", 3), ("load1", 3), ("bias_a", 3), ("mid_a", K),
    ("ping_a", 3), ("pong_a", 3), ("full_a", 0),
)


def kernel(temp_hbm, visc_hbm, pinned_hbm, loads_hbm, out_hbm, *scratch):
    fields = {name: Field(ref, margin) for (name, margin), ref in zip(MARGINS, scratch)}
    coef1, coef2, send_sem, recv_sem, in_sem, out_sem = scratch[len(MARGINS):]
    temp, visc, pinned, half, weight, bias, ping, pong, mid, full, mid2 = (
        fields[name] for name, _ in MARGINS[:11]
    )
    load0, load1, bias_a, mid_a, ping_a, pong_a, full_a = (fields[name] for name, _ in MARGINS[11:])

    role, rad, lat = (lax.axis_index(name) for name in ("role", "rad", "lat"))
    peers = lax.axis_size("lat")
    left = (role, rad, lax.rem(lat + peers - 1, peers))
    right = (role, rad, lax.rem(lat + 1, peers))
    core = (role, 1 - rad, lat)
    is_forward = role == 0
    own = 1 + (H - 1) * rad

    barrier = pltpu.get_barrier_semaphore()
    for device in (left, right, core):
        pl.semaphore_signal(barrier, inc=1, device_id=device, device_id_type=MESH)

    def arriving(source, field, which):
        return [
            pltpu.make_async_copy(
                source.at[:, :, pl.ds(128 * j, 128)],
                field.ref.at[pl.ds(own, N), pl.ds(field.margin, N), j, :],
                in_sem.at[which, j],
            )
            for j in range(8)
        ]

    loading = [
        arriving(temp_hbm, temp, 0),
        arriving(visc_hbm, visc, 1),
        arriving(pinned_hbm, pinned, 2),
    ]
    loading_adjoint = [
        arriving(loads_hbm.at[0], load0, 3),
        arriving(loads_hbm.at[1], load1, 4),
    ]
    for copies in loading:
        for copy in copies:
            copy.start()

    @pl.when(role == 1)
    def _():
        for copies in loading_adjoint:
            for copy in copies:
                copy.start()

    outside = (ROWS - 1) * rad
    for field in (temp, half, bias, ping, pong, mid, full, mid2, bias_a, mid_a, ping_a, pong_a):
        field.ref[outside] = jnp.zeros((N + 2 * field.margin, 8, 128), jnp.float32)

    def first_row(low, high):
        return own + (1 - rad) * low + rad * (N - high)

    def remote(field, which, part, rows_from, rows_to, rows, l_from, l_to, layers, device):
        return pltpu.make_async_remote_copy(
            src_ref=field.view(rows_from, rows, l_from, layers),
            dst_ref=field.view(rows_to, rows, l_to, layers),
            send_sem=send_sem.at[which, part],
            recv_sem=recv_sem.at[which, part],
            device_id=device,
            device_id_type=MESH,
        )

    def margins(field, which):
        d = DEPTH[which]
        rows = H if which in (T, FAR) else d
        skip = K if which == FAR else 0
        rows_from = (1 - rad) * (1 + N - rows) + rad * H
        rows_to = (1 - rad) * (H - rows) + rad * (1 + N)
        before, after = -skip - d, N + skip
        parts = {
            CORNER_LEFT: remote(field, which, CORNER_LEFT, rows_from, rows_to, rows, before, before, d, core),
            CORNER_RIGHT: remote(field, which, CORNER_RIGHT, rows_from, rows_to, rows, after, after, d, core),
        }
        if which != FAR:
            parts[CORE] = remote(field, which, CORE, rows_from, rows_to, rows, 0, 0, N, core)
        high = N
        for i, low in enumerate(CHUNKS.get(which, WHOLE)):
            row, rows = first_row(low, high), high - low
            parts[LEFT + i] = remote(field, which, LEFT + i, row, row, rows, skip, after, d, left)
            parts[RIGHT + i] = remote(field, which, RIGHT + i, row, row, rows, N - skip - d, before, d, right)
            high = low
        return parts

    moves = {
        which: margins(field, which)
        for which, field in (
            (T, temp), (V, visc), (M, pinned), (L0, load0), (L1, load1),
            (F4, mid), (A4, mid_a), (F8, full), (G4, mid2), (FAR, temp),
        )
    }

    def send_core(which):
        moves[which][CORE].start()

    def send_chunk(which, i):
        moves[which][LEFT + i].start()
        moves[which][RIGHT + i].start()

    def have_core(*these):
        for which in these:
            moves[which][CORE].wait_recv()

    def have_chunk(i, *these):
        for which in these:
            moves[which][LEFT + i].wait_recv()
            moves[which][RIGHT + i].wait_recv()

    def send_corners(*these):
        for which in these:
            moves[which][CORNER_LEFT].start()
            moves[which][CORNER_RIGHT].start()

    def have_corners(*these):
        for which in these:
            moves[which][CORNER_LEFT].wait_recv()
            moves[which][CORNER_RIGHT].wait_recv()

    def have_sides(which):
        have_chunk(0, which)
        send_corners(which)
        have_corners(which)

    def sent(*these):
        for which in these:
            for move in moves[which].values():
                move.wait_send()

    first, last, bottom, top = b_masks()

    def over(low, high, spans, body):
        if high - low <= 11 or (high - low) % 2 and high == N + K:
            groups = 1
        else:
            groups = 2
            high += (high - low) % 2
        group = (high - low) // groups
        start = first_row(low, high)

        def rows(g, carry):
            def row(i, inner):
                for begin, end in spans:
                    l = begin
                    while l < end:
                        n = min(end - l, 8)
                        body(start + g * group + i, l, n)
                        l += n
                return inner

            return lax.fori_loop(0, group, row, carry, unroll=True)

        if groups == 1:
            rows(0, 0)
        else:
            lax.fori_loop(0, groups, rows, 0)

    def sweep(source, target, forced, coef, spans):
        def body(r, l, n):
            here = pl.ds(3 + l, n)
            centre = source.get(r, l, n)
            total = forced.get(r, l, n) + coef[0, r, here] * source.get(r + 1, l, n)
            total = total + coef[1, r, here] * source.get(r - 1, l, n)
            total = total + coef[2, r, here] * source.get(r, l + 1, n)
            total = total + coef[3, r, here] * source.get(r, l - 1, n)
            total = total + coef[4, r, here] * above(centre, last)
            total = total + coef[5, r, here] * below(centre, first)
            target.put(r, l, total)

        return lambda low, high: over(low, high, spans, body)

    def halves(field, spans):
        def body(r, l, n):
            half.put(r, l, 0.5 * visc.get(r, l, n) * jnp.exp(-SOFTENING * field.get(r, l, n)))

        return lambda low, high: over(low, high, spans, body)

    def couplings(field, coef, spans, pick):
        def body(r, l, n):
            here = pl.ds(3 + l, n)
            centre = half.get(r, l, n)
            around = (
                half.get(r + 1, l, n),
                half.get(r - 1, l, n),
                half.get(r, l + 1, n),
                half.get(r, l - 1, n),
                jnp.where(top, 0.0, above(centre, last)),
                jnp.where(bottom, 0.0, below(centre, first)),
            )
            diagonal = 7.0 * centre
            for other in around:
                diagonal = diagonal + other
            held = pinned.get(r, l, n).astype(jnp.float32)
            scale = (1.0 - held) / (diagonal + held)
            for i, other in enumerate(around):
                value = scale * (centre + other)
                if i == 4:
                    value = jnp.where(top, 0.0, value)
                if i == 5:
                    value = jnp.where(bottom, 0.0, value)
                coef[i, r, here] = value
            forcing = (0.5 * RAYLEIGH) * (field.get(r, l + 1, n) - field.get(r, l - 1, n))
            if pick:
                forcing = jnp.where(is_forward, forcing, load1.get(r, l, n))
            else:
                weight.put(r, l, scale)
            bias.put(r, l, scale * forcing)

        return lambda low, high: over(low, high, spans, body)

    def adjoint_bias(spans):
        def body(r, l, n):
            bias_a.put(r, l, weight.get(r, l, n) * load0.get(r, l, n))

        return lambda low, high: over(low, high, spans, body)

    def advance(target, spans):
        def body(r, l, n):
            centre = temp.get(r, l, n)
            r_up, r_down = temp.get(r + 1, l, n), temp.get(r - 1, l, n)
            l_up, l_down = temp.get(r, l + 1, n), temp.get(r, l - 1, n)
            laplace = r_up + r_down + l_up + l_down
            laplace = laplace + jnp.where(top, 0.0, above(centre, last))
            laplace = laplace + jnp.where(bottom, 0.0, below(centre, first)) - 6.0 * centre
            radial = full.get(r, l + 1, n) - full.get(r, l - 1, n)
            lateral = full.get(r + 1, l, n) - full.get(r - 1, l, n)
            transport = 0.25 * (radial * (r_up - r_down) - lateral * (l_up - l_down))
            target.put(r, l, centre + TIME_STEP * (laplace - transport))

        return lambda low, high: over(low, high, spans, body)

    def middle(j, shift=0):
        return ((j + shift, N - j - shift),)

    def sides(j, shift=0):
        return ((j - K, j + shift), (N - j - shift, N + K - j))

    def first_half(x, y, result, forced, coef, spans, lag):
        return [
            (sweep(source, target, forced, coef, spans(j)), lag + j, N + K - j)
            for j, source, target in ((2, forced, x), (3, x, y), (4, y, result))
        ]

    def second_half(begin, x, y, result, forced, coef, spans):
        return [
            (sweep(source, target, forced, coef, spans(j)), j, N + K - j)
            for j, source, target in ((1, begin, x), (2, x, y), (3, y, x), (4, x, result))
        ]

    def all_rows(stage):
        for work, _, high in stage:
            work(0, high)

    def wave(stage, arrive, leave, steps=STEPS):
        highs = [high for _, _, high in stage]
        for i, low in enumerate(steps):
            arrive(i)
            if i == 0:
                continue
            for place, (work, lag, _) in enumerate(stage):
                begin = min(low + lag, highs[place]) if low else 0
                if begin < highs[place]:
                    work(begin, highs[place])
                    highs[place] = begin
            leave(i)

    def writing(field, which, part, low, high):
        row = first_row(low, high)
        return pltpu.make_async_copy(
            field.view(row, high - low, 0, N),
            out_hbm.at[which, pl.ds(row - own, high - low)],
            out_sem.at[which, part],
        )

    for copies in loading:
        for copy in copies:
            copy.wait()
    pl.semaphore_wait(barrier, 3)
    for i in range(len(STEPS)):
        for which in (T, V, M):
            send_chunk(which, i)
        if i == 0:
            for which in (T, V, M):
                send_core(which)

    @pl.when(role == 1)
    def _():
        for copies in loading_adjoint:
            for copy in copies:
                copy.wait()
        send_chunk(L0, 0)
        send_core(L0)
        send_core(L1)

    have_core(T, V, M)
    all_rows(
        [(halves(temp, ((0, N),)), 0, N + K), (couplings(temp, coef1, middle(1), False), 1, N + K - 1)]
        + first_half(ping, pong, mid, bias, coef1, middle, 0)
    )

    def inputs_arrive(i):
        have_chunk(i, T, V, M)
        if i == 0:
            send_corners(T, V, M)
        if i == 1:
            have_corners(T, V, M)

    def leave_four(which):
        def leave(i):
            if i == 1:
                send_chunk(which, 0)
                send_core(which)
            if i == 2:
                send_chunk(which, 1)
            if i == 3:
                send_chunk(which, 2)
                send_chunk(which, 3)

        return leave

    wave(
        [(halves(temp, ((-K, 0), (N, N + K))), 0, N + K), (couplings(temp, coef1, sides(1), False), 1, N + K - 1)]
        + first_half(ping, pong, mid, bias, coef1, sides, 0),
        inputs_arrive,
        leave_four(F4),
    )

    send_chunk(FAR, 0)

    @pl.when(role == 1)
    def _():
        send_chunk(L1, 0)

    have_core(F4)
    all_rows(second_half(mid, ping, pong, full, bias, coef1, middle))

    @pl.when(role == 1)
    def _():
        have_core(L0, L1)
        all_rows(
            [(adjoint_bias(middle(1)), 0, N + K - 1)]
            + first_half(ping_a, pong_a, mid_a, bias_a, coef1, middle, 0)
        )
        have_sides(L0)
        all_rows(
            [(adjoint_bias(sides(1)), 0, N + K - 1)]
            + first_half(ping_a, pong_a, mid_a, bias_a, coef1, sides, 0)
        )

    def potential_arrives(which):
        def arrive(i):
            have_chunk(i, which)
            if i == 0:
                send_corners(which)
            if i == 1:
                have_corners(which)

        return arrive

    def leave_full(i):
        if i == 1:
            send_chunk(F8, 0)
            send_core(F8)
        if i == 2:
            send_chunk(F8, 1)
        if i == 3:
            send_chunk(F8, 2)
            send_chunk(F8, 3)

    wave(second_half(mid, ping, pong, full, bias, coef1, sides), potential_arrives(F4), leave_full)

    @pl.when(role == 0)
    def _():
        writing(full, 0, 0, 0, N).start()

    @pl.when(role == 1)
    def _():
        send_chunk(A4, 0)
        send_core(A4)

    sent(F4)
    temp_next = mid
    have_core(F8)
    all_rows(
        [
            (advance(temp_next, middle(1)), 0, N + K),
            (halves(temp_next, middle(1)), 0, N + K),
            (couplings(temp_next, coef2, middle(2), True), 0, N + K - 1),
        ]
        + first_half(ping, pong, mid2, bias, coef2, lambda j: middle(j, 1), 0)
    )
    have_sides(FAR)

    @pl.when(role == 1)
    def _():
        have_sides(L1)

    def full_arrives(i):
        have_chunk(i, F8)
        if i == 1:
            send_corners(F8)
            have_corners(F8)

    def leave_next(i):
        if i == 1:
            send_chunk(G4, 0)
            send_core(G4)
        if i == 2:
            send_chunk(G4, 1)
        if i == 3:
            send_chunk(G4, 2)
            send_chunk(G4, 3)

    wave(
        [
            (advance(temp_next, ((-K, 1), (N - 1, N + K))), 1, N + K),
            (halves(temp_next, ((-K, 1), (N - 1, N + K))), 1, N + K),
            (couplings(temp_next, coef2, sides(1, 1), True), 2, N + K - 1),
        ]
        + first_half(ping, pong, mid2, bias, coef2, lambda j: sides(j, 1), 1),
        full_arrives,
        leave_next,
    )
    final = temp
    sent(T, V, M, FAR)
    have_core(G4)
    all_rows(second_half(mid2, ping, pong, final, bias, coef2, middle))

    @pl.when(role == 1)
    def _():
        have_core(A4)
        all_rows(second_half(mid_a, ping_a, pong_a, full_a, bias_a, coef1, middle))
        have_sides(A4)
        all_rows(second_half(mid_a, ping_a, pong_a, full_a, bias_a, coef1, sides))
        writing(full_a, 0, 0, 0, N).start()

    def leave_final(i):
        if i == 2:
            writing(final, 1, 0, 6, N).start()
        if i == 3:
            writing(final, 1, 1, 0, 6).start()

    wave(second_half(mid2, ping, pong, final, bias, coef2, sides), potential_arrives(G4), leave_final, LATER)
    sent(F8, G4)

    @pl.when(role == 1)
    def _():
        sent(L0, L1, A4)

    writing(full, 0, 0, 0, N).wait()
    writing(final, 1, 0, 6, N).wait()
    writing(final, 1, 1, 0, 6).wait()


def per_device(temp_start, visc_ref, pinned, loads):
    def block(margin, dtype=jnp.float32, lead=()):
        return pltpu.VMEM(lead + (ROWS, N + 2 * margin, 8, 128), dtype)

    scratch = [block(margin, jnp.int32 if name == "pinned" else jnp.float32) for name, margin in MARGINS]
    scratch += [block(3, lead=(6,)), block(3, lead=(6,))]
    scratch += [
        pltpu.SemaphoreType.DMA((10, 11)),
        pltpu.SemaphoreType.DMA((10, 11)),
        pltpu.SemaphoreType.DMA((5, 8)),
        pltpu.SemaphoreType.DMA((2, 2)),
    ]
    result = pl.pallas_call(
        kernel,
        out_shape=jax.ShapeDtypeStruct((2, N, N, 8, 128), jnp.float32),
        in_specs=[pl.BlockSpec(memory_space=pl.ANY)] * 4,
        out_specs=pl.BlockSpec(memory_space=pl.ANY),
        scratch_shapes=scratch,
        compiler_params=pltpu.CompilerParams(
            collective_id=0, has_side_effects=True, vmem_limit_bytes=60 * 1024 * 1024
        ),
    )(temp_start, visc_ref, pinned, loads)
    return result.reshape(1, 2, N, N, 1024)


def solution(mesh):
    in_specs = (
        P("rad", "lat", None),
        P("rad", "lat", None),
        P("rad", "lat", None),
        P(None, "rad", "lat", None),
    )
    out_specs = P("role", None, "rad", "lat", None)
    return jax.shard_map(
        per_device, mesh=mesh, in_specs=in_specs, out_specs=out_specs, check_vma=False
    )
```

```python
import jax
import jax.numpy as jnp
from jax import lax
from jax.experimental import pallas as pl
from jax.experimental.pallas import tpu as pltpu
from jax.sharding import PartitionSpec as P

MESH = pl.DeviceIdType.MESH
TIME_STEP = 0.1
SOFTENING = 2.0
RAYLEIGH = 8.0

K = 4
H = K + 1
N = 16
ROWS = N + H + 1

T, V, M, L0, L1, F4, A4, F8, G4, FAR = range(10)
DEPTH = {T: K, V: K, M: K - 1, L0: K - 1, L1: K - 1, F4: K, A4: K, F8: H, G4: K, FAR: 1}
STEPS = (12, 6, 2, 0)
LATER = (12, 7, 2, 0)
WHOLE = (0,)
CHUNKS = {T: (11, 6, 2, 0), V: STEPS, M: STEPS, F4: STEPS, F8: STEPS, G4: LATER}
CORE, CORNER_LEFT, CORNER_RIGHT, LEFT, RIGHT = 0, 1, 2, 3, 7


def b_masks():
    lane = lax.broadcasted_iota(jnp.int32, (1, 8, 128), 2)
    sub = lax.broadcasted_iota(jnp.int32, (1, 8, 128), 1)
    first, last = lane == 0, lane == 127
    return first, last, first & (sub == 0), last & (sub == 7)


def above(x, last):
    rolled = pltpu.roll(x, 127, 2)
    return jnp.where(last, pltpu.roll(rolled, 7, 1), rolled)


def below(x, first):
    rolled = pltpu.roll(x, 1, 2)
    return jnp.where(first, pltpu.roll(rolled, 1, 1), rolled)


class Field:
    def __init__(self, ref, margin):
        self.ref, self.margin = ref, margin

    def get(self, r, l, n):
        return self.ref[r, pl.ds(self.margin + l, n)]

    def put(self, r, l, value):
        self.ref[r, pl.ds(self.margin + l, value.shape[0])] = value

    def view(self, r, rows, l, layers):
        return self.ref.at[pl.ds(r, rows), pl.ds(self.margin + l, layers)]


MARGINS = (
    ("temp", H), ("visc", K), ("pinned", 3), ("half", K), ("weight", 3), ("bias", 3), ("ping", 3), ("pong", 3),
    ("mid", K), ("full", H), ("mid2", K), ("load0", 3), ("load1", 3), ("bias_a", 3), ("mid_a", K),
    ("ping_a", 3), ("pong_a", 3), ("full_a", 0),
)


def kernel(temp_hbm, visc_hbm, pinned_hbm, loads_hbm, out_hbm, *scratch):
    fields = {name: Field(ref, margin) for (name, margin), ref in zip(MARGINS, scratch)}
    coef1, coef2, send_sem, recv_sem, in_sem, out_sem = scratch[len(MARGINS):]
    temp, visc, pinned, half, weight, bias, ping, pong, mid, full, mid2 = (
        fields[name] for name, _ in MARGINS[:11]
    )
    load0, load1, bias_a, mid_a, ping_a, pong_a, full_a = (fields[name] for name, _ in MARGINS[11:])

    role, rad, lat = (lax.axis_index(name) for name in ("role", "rad", "lat"))
    peers = lax.axis_size("lat")
    left = (role, rad, lax.rem(lat + peers - 1, peers))
    right = (role, rad, lax.rem(lat + 1, peers))
    core = (role, 1 - rad, lat)
    is_forward = role == 0
    own = 1 + (H - 1) * rad

    barrier = pltpu.get_barrier_semaphore()
    for device in (left, right, core):
        pl.semaphore_signal(barrier, inc=1, device_id=device, device_id_type=MESH)

    def arriving(source, field, which):
        return [
            pltpu.make_async_copy(
                source.at[:, :, pl.ds(128 * j, 128)],
                field.ref.at[pl.ds(own, N), pl.ds(field.margin, N), j, :],
                in_sem.at[which, j],
            )
            for j in range(8)
        ]

    loading = [
        arriving(temp_hbm, temp, 0),
        arriving(visc_hbm, visc, 1),
        arriving(pinned_hbm, pinned, 2),
    ]
    loading_adjoint = [
        arriving(loads_hbm.at[0], load0, 3),
        arriving(loads_hbm.at[1], load1, 4),
    ]
    for copies in loading:
        for copy in copies:
            copy.start()

    @pl.when(role == 1)
    def _():
        for copies in loading_adjoint:
            for copy in copies:
                copy.start()

    outside = (ROWS - 1) * rad
    for field in (temp, half, bias, ping, pong, mid, full, mid2, bias_a, mid_a, ping_a, pong_a):
        field.ref[outside] = jnp.zeros((N + 2 * field.margin, 8, 128), jnp.float32)

    def first_row(low, high):
        return own + (1 - rad) * low + rad * (N - high)

    def remote(field, which, part, rows_from, rows_to, rows, l_from, l_to, layers, device):
        return pltpu.make_async_remote_copy(
            src_ref=field.view(rows_from, rows, l_from, layers),
            dst_ref=field.view(rows_to, rows, l_to, layers),
            send_sem=send_sem.at[which, part],
            recv_sem=recv_sem.at[which, part],
            device_id=device,
            device_id_type=MESH,
        )

    def margins(field, which):
        d = DEPTH[which]
        rows = H if which in (T, FAR) else d
        skip = K if which == FAR else 0
        rows_from = (1 - rad) * (1 + N - rows) + rad * H
        rows_to = (1 - rad) * (H - rows) + rad * (1 + N)
        before, after = -skip - d, N + skip
        parts = {
            CORNER_LEFT: remote(field, which, CORNER_LEFT, rows_from, rows_to, rows, before, before, d, core),
            CORNER_RIGHT: remote(field, which, CORNER_RIGHT, rows_from, rows_to, rows, after, after, d, core),
        }
        if which != FAR:
            parts[CORE] = remote(field, which, CORE, rows_from, rows_to, rows, 0, 0, N, core)
        high = N
        for i, low in enumerate(CHUNKS.get(which, WHOLE)):
            row, rows = first_row(low, high), high - low
            parts[LEFT + i] = remote(field, which, LEFT + i, row, row, rows, skip, after, d, left)
            parts[RIGHT + i] = remote(field, which, RIGHT + i, row, row, rows, N - skip - d, before, d, right)
            high = low
        return parts

    moves = {
        which: margins(field, which)
        for which, field in (
            (T, temp), (V, visc), (M, pinned), (L0, load0), (L1, load1),
            (F4, mid), (A4, mid_a), (F8, full), (G4, mid2), (FAR, temp),
        )
    }

    def send_core(which):
        moves[which][CORE].start()

    def send_chunk(which, i):
        moves[which][LEFT + i].start()
        moves[which][RIGHT + i].start()

    def have_core(*these):
        for which in these:
            moves[which][CORE].wait_recv()

    def have_chunk(i, *these):
        for which in these:
            moves[which][LEFT + i].wait_recv()
            moves[which][RIGHT + i].wait_recv()

    def send_corners(*these):
        for which in these:
            moves[which][CORNER_LEFT].start()
            moves[which][CORNER_RIGHT].start()

    def have_corners(*these):
        for which in these:
            moves[which][CORNER_LEFT].wait_recv()
            moves[which][CORNER_RIGHT].wait_recv()

    def have_sides(which):
        have_chunk(0, which)
        send_corners(which)
        have_corners(which)

    def sent(*these):
        for which in these:
            for move in moves[which].values():
                move.wait_send()

    first, last, bottom, top = b_masks()

    def over(low, high, spans, body):
        if high - low <= 11 or (high - low) % 2 and high == N + K:
            groups = 1
        else:
            groups = 2
            high += (high - low) % 2
        group = (high - low) // groups
        start = first_row(low, high)

        def rows(g, carry):
            def row(i, inner):
                for begin, end in spans:
                    l = begin
                    while l < end:
                        n = min(end - l, 8)
                        body(start + g * group + i, l, n)
                        l += n
                return inner

            return lax.fori_loop(0, group, row, carry, unroll=True)

        if groups == 1:
            rows(0, 0)
        else:
            lax.fori_loop(0, groups, rows, 0)

    def sweep(source, target, forced, coef, spans):
        def body(r, l, n):
            here = pl.ds(3 + l, n)
            centre = source.get(r, l, n)
            total = forced.get(r, l, n) + coef[0, r, here] * source.get(r + 1, l, n)
            total = total + coef[1, r, here] * source.get(r - 1, l, n)
            total = total + coef[2, r, here] * source.get(r, l + 1, n)
            total = total + coef[3, r, here] * source.get(r, l - 1, n)
            total = total + coef[4, r, here] * above(centre, last)
            total = total + coef[5, r, here] * below(centre, first)
            target.put(r, l, total)

        return lambda low, high: over(low, high, spans, body)

    def halves(field, spans):
        def body(r, l, n):
            half.put(r, l, 0.5 * visc.get(r, l, n) * jnp.exp(-SOFTENING * field.get(r, l, n)))

        return lambda low, high: over(low, high, spans, body)

    def couplings(field, coef, spans, pick):
        def body(r, l, n):
            here = pl.ds(3 + l, n)
            centre = half.get(r, l, n)
            around = (
                half.get(r + 1, l, n),
                half.get(r - 1, l, n),
                half.get(r, l + 1, n),
                half.get(r, l - 1, n),
                jnp.where(top, 0.0, above(centre, last)),
                jnp.where(bottom, 0.0, below(centre, first)),
            )
            diagonal = 7.0 * centre
            for other in around:
                diagonal = diagonal + other
            held = pinned.get(r, l, n).astype(jnp.float32)
            scale = (1.0 - held) / (diagonal + held)
            for i, other in enumerate(around):
                value = scale * (centre + other)
                if i == 4:
                    value = jnp.where(top, 0.0, value)
                if i == 5:
                    value = jnp.where(bottom, 0.0, value)
                coef[i, r, here] = value
            forcing = (0.5 * RAYLEIGH) * (field.get(r, l + 1, n) - field.get(r, l - 1, n))
            if pick:
                forcing = jnp.where(is_forward, forcing, load1.get(r, l, n))
            else:
                weight.put(r, l, scale)
            bias.put(r, l, scale * forcing)

        return lambda low, high: over(low, high, spans, body)

    def adjoint_bias(spans):
        def body(r, l, n):
            bias_a.put(r, l, weight.get(r, l, n) * load0.get(r, l, n))

        return lambda low, high: over(low, high, spans, body)

    def advance(target, spans):
        def body(r, l, n):
            centre = temp.get(r, l, n)
            r_up, r_down = temp.get(r + 1, l, n), temp.get(r - 1, l, n)
            l_up, l_down = temp.get(r, l + 1, n), temp.get(r, l - 1, n)
            laplace = r_up + r_down + l_up + l_down
            laplace = laplace + jnp.where(top, 0.0, above(centre, last))
            laplace = laplace + jnp.where(bottom, 0.0, below(centre, first)) - 6.0 * centre
            radial = full.get(r, l + 1, n) - full.get(r, l - 1, n)
            lateral = full.get(r + 1, l, n) - full.get(r - 1, l, n)
            transport = 0.25 * (radial * (r_up - r_down) - lateral * (l_up - l_down))
            target.put(r, l, centre + TIME_STEP * (laplace - transport))

        return lambda low, high: over(low, high, spans, body)

    def middle(j, shift=0):
        return ((j + shift, N - j - shift),)

    def sides(j, shift=0):
        return ((j - K, j + shift), (N - j - shift, N + K - j))

    def first_half(x, y, result, forced, coef, spans, lag):
        return [
            (sweep(source, target, forced, coef, spans(j)), lag + j, N + K - j)
            for j, source, target in ((2, forced, x), (3, x, y), (4, y, result))
        ]

    def second_half(begin, x, y, result, forced, coef, spans):
        return [
            (sweep(source, target, forced, coef, spans(j)), j, N + K - j)
            for j, source, target in ((1, begin, x), (2, x, y), (3, y, x), (4, x, result))
        ]

    def all_rows(stage):
        for work, _, high in stage:
            work(0, high)

    def wave(stage, arrive, leave, steps=STEPS):
        highs = [high for _, _, high in stage]
        for i, low in enumerate(steps):
            arrive(i)
            if i == 0:
                continue
            for place, (work, lag, _) in enumerate(stage):
                begin = min(low + lag, highs[place]) if low else 0
                if begin < highs[place]:
                    work(begin, highs[place])
                    highs[place] = begin
            leave(i)

    def writing(field, which, part, low, high):
        row = first_row(low, high)
        return pltpu.make_async_copy(
            field.view(row, high - low, 0, N),
            out_hbm.at[which, pl.ds(row - own, high - low)],
            out_sem.at[which, part],
        )

    for copies in loading:
        for copy in copies:
            copy.wait()
    pl.semaphore_wait(barrier, 3)
    for i in range(len(STEPS)):
        for which in (T, V, M):
            send_chunk(which, i)
        if i == 0:
            for which in (T, V, M):
                send_core(which)

    @pl.when(role == 1)
    def _():
        for copies in loading_adjoint:
            for copy in copies:
                copy.wait()
        send_chunk(L0, 0)
        send_core(L0)
        send_core(L1)

    have_core(T, V, M)
    all_rows(
        [(halves(temp, ((0, N),)), 0, N + K), (couplings(temp, coef1, middle(1), False), 1, N + K - 1)]
        + first_half(ping, pong, mid, bias, coef1, middle, 0)
    )

    def inputs_arrive(i):
        have_chunk(i, T, V, M)
        if i == 0:
            send_corners(T, V, M)
        if i == 1:
            have_corners(T, V, M)

    def leave_four(which):
        def leave(i):
            if i == 1:
                send_chunk(which, 0)
                send_core(which)
            if i == 2:
                send_chunk(which, 1)
            if i == 3:
                send_chunk(which, 2)
                send_chunk(which, 3)

        return leave

    wave(
        [(halves(temp, ((-K, 0), (N, N + K))), 0, N + K), (couplings(temp, coef1, sides(1), False), 1, N + K - 1)]
        + first_half(ping, pong, mid, bias, coef1, sides, 0),
        inputs_arrive,
        leave_four(F4),
    )

    send_chunk(FAR, 0)

    @pl.when(role == 1)
    def _():
        send_chunk(L1, 0)

    have_core(F4)
    all_rows(second_half(mid, ping, pong, full, bias, coef1, middle))

    @pl.when(role == 1)
    def _():
        have_core(L0, L1)
        all_rows(
            [(adjoint_bias(middle(1)), 0, N + K - 1)]
            + first_half(ping_a, pong_a, mid_a, bias_a, coef1, middle, 0)
        )
        have_sides(L0)
        all_rows(
            [(adjoint_bias(sides(1)), 0, N + K - 1)]
            + first_half(ping_a, pong_a, mid_a, bias_a, coef1, sides, 0)
        )

    def potential_arrives(which):
        def arrive(i):
            have_chunk(i, which)
            if i == 0:
                send_corners(which)
            if i == 1:
                have_corners(which)

        return arrive

    def leave_full(i):
        if i == 1:
            send_chunk(F8, 0)
            send_core(F8)
        if i == 2:
            send_chunk(F8, 1)
        if i == 3:
            send_chunk(F8, 2)
            send_chunk(F8, 3)

    wave(second_half(mid, ping, pong, full, bias, coef1, sides), potential_arrives(F4), leave_full)

    @pl.when(role == 0)
    def _():
        writing(full, 0, 0, 0, N).start()

    @pl.when(role == 1)
    def _():
        send_chunk(A4, 0)
        send_core(A4)

    sent(F4)
    temp_next = mid
    have_core(F8)
    all_rows(
        [
            (advance(temp_next, middle(1)), 0, N + K),
            (halves(temp_next, middle(1)), 0, N + K),
            (couplings(temp_next, coef2, middle(2), True), 0, N + K - 1),
        ]
        + first_half(ping, pong, mid2, bias, coef2, lambda j: middle(j, 1), 0)
    )
    have_sides(FAR)

    @pl.when(role == 1)
    def _():
        have_sides(L1)

    def full_arrives(i):
        have_chunk(i, F8)
        if i == 1:
            send_corners(F8)
            have_corners(F8)

    def leave_next(i):
        if i == 1:
            send_chunk(G4, 0)
            send_core(G4)
        if i == 2:
            send_chunk(G4, 1)
        if i == 3:
            send_chunk(G4, 2)
            send_chunk(G4, 3)

    wave(
        [
            (advance(temp_next, ((-K, 1), (N - 1, N + K))), 1, N + K),
            (halves(temp_next, ((-K, 1), (N - 1, N + K))), 1, N + K),
            (couplings(temp_next, coef2, sides(1, 1), True), 2, N + K - 1),
        ]
        + first_half(ping, pong, mid2, bias, coef2, lambda j: sides(j, 1), 1),
        full_arrives,
        leave_next,
    )
    final = temp
    sent(T, V, M, FAR)
    have_core(G4)
    all_rows(second_half(mid2, ping, pong, final, bias, coef2, middle))

    @pl.when(role == 1)
    def _():
        have_core(A4)
        all_rows(second_half(mid_a, ping_a, pong_a, full_a, bias_a, coef1, middle))

    def adjoint_sides():
        @pl.when(role == 1)
        def _():
            have_sides(A4)
            all_rows(second_half(mid_a, ping_a, pong_a, full_a, bias_a, coef1, sides))
            writing(full_a, 0, 0, 0, N).start()

    def leave_final(i):
        if i == 1:
            adjoint_sides()
        if i == 2:
            writing(final, 1, 0, 6, N).start()
        if i == 3:
            writing(final, 1, 1, 0, 6).start()

    wave(second_half(mid2, ping, pong, final, bias, coef2, sides), potential_arrives(G4), leave_final, LATER)
    sent(F8, G4)

    @pl.when(role == 1)
    def _():
        sent(L0, L1, A4)

    writing(full, 0, 0, 0, N).wait()
    writing(final, 1, 0, 6, N).wait()
    writing(final, 1, 1, 0, 6).wait()


def per_device(temp_start, visc_ref, pinned, loads):
    def block(margin, dtype=jnp.float32, lead=()):
        return pltpu.VMEM(lead + (ROWS, N + 2 * margin, 8, 128), dtype)

    scratch = [block(margin, jnp.int32 if name == "pinned" else jnp.float32) for name, margin in MARGINS]
    scratch += [block(3, lead=(6,)), block(3, lead=(6,))]
    scratch += [
        pltpu.SemaphoreType.DMA((10, 11)),
        pltpu.SemaphoreType.DMA((10, 11)),
        pltpu.SemaphoreType.DMA((5, 8)),
        pltpu.SemaphoreType.DMA((2, 2)),
    ]
    result = pl.pallas_call(
        kernel,
        out_shape=jax.ShapeDtypeStruct((2, N, N, 8, 128), jnp.float32),
        in_specs=[pl.BlockSpec(memory_space=pl.ANY)] * 4,
        out_specs=pl.BlockSpec(memory_space=pl.ANY),
        scratch_shapes=scratch,
        compiler_params=pltpu.CompilerParams(
            collective_id=0, has_side_effects=True, vmem_limit_bytes=60 * 1024 * 1024
        ),
    )(temp_start, visc_ref, pinned, loads)
    return result.reshape(1, 2, N, N, 1024)


def solution(mesh):
    in_specs = (
        P("rad", "lat", None),
        P("rad", "lat", None),
        P("rad", "lat", None),
        P(None, "rad", "lat", None),
    )
    out_specs = P("role", None, "rad", "lat", None)
    return jax.shard_map(
        per_device, mesh=mesh, in_specs=in_specs, out_specs=out_specs, check_vma=False
    )
```
